256 devices in a mesh: seq: 8 (over z), head: 32 (over x, y, core).
Axes of the slice: x: 4, y: 4, z: 8, core: 2. Of those that a mesh axis runs over, the one named last changes fastest.
Arguments:
- projected: bfloat16 [2, 16384, 16384], P(None, ('seq', 'head')), may hold values from -6 to 6
- state_maps: bfloat16 [2, 16384, 4096], P(None, ('seq', 'head')), may hold values from -3 to 3
- step_raw: bfloat16 [2, 16384, 256], P(None, ('seq', 'head')), may hold values from -3 to 14
- step_bias: float32 [256], P('head'), may hold values from -9 to -2
- decay_rate: float32 [256], P('head'), may hold values from 0.1 to 2
- skip_gain: float32 [256], P('head'), may hold values from 0.5 to 1.5
- conv_weight: bfloat16 [4, 16384], P(None, 'head'), may hold values from -3 to 3
- conv_bias: float32 [16384], P('head'), may hold values from -1.5 to 1.5
- map_weight: bfloat16 [4, 4096], replicated, may hold values from -3 to 3
- map_bias: float32 [4096], replicated, may hold values from -1.5 to 1.5
Outputs:
- mixed_out: bfloat16 [2, 16384, 16384], P(None, ('seq', 'head'))
The draws below stay inside these ranges and needn't reach their ends.
All inputs are finite; a program needn't handle non-finite values.
Results may differ from the reference program's by a relative error of at most 0.0057.
Values may be sent and summed in bfloat16 or wider, within the bound.
A program may use at most 128 MiB of HBM per device.

```python
import jax
import jax.numpy as jnp
from jax import lax

HEADS = 256
HEAD_DIM = 64
STATE = 256
GROUPS = 8
SPAN = 256
CONV = 4
SEQS = 2
DI = 16384
LEN = 16384


def head_law(key):
    keys = jax.random.split(jax.random.fold_in(key, 11), 4)
    share = 0.5
    slow = jax.random.bernoulli(keys[0], share, (HEADS,))
    slow_rate = jnp.exp(jax.random.uniform(keys[1], (HEADS,), jnp.float32, jnp.log(0.1), jnp.log(0.25)))
    fast_rate = jnp.exp(jax.random.uniform(keys[2], (HEADS,), jnp.float32, jnp.log(0.5), jnp.log(2.0)))
    fast_step = jnp.exp(jax.random.uniform(keys[3], (HEADS,), jnp.float32, jnp.log(1.0 / 50.0), jnp.log(1.0 / 30.0)))
    rate_entry = jnp.where(slow, slow_rate, fast_rate)
    step_value = jnp.where(slow, 1.5 / LEN, fast_step)
    offset_bias_entry = jnp.log(jnp.expm1(step_value / rate_entry))
    return (rate_entry, offset_bias_entry)


def draw_decay_rate(key, part):
    return head_law(key)[0]


def draw_step_bias(key, part):
    return head_law(key)[1]


def draw_step_raw(key, part):
    rate_entry, offset_bias_entry = head_law(key)
    keys = jax.random.split(jax.random.fold_in(key, 23), 3)
    noise = 0.6 * jax.random.truncated_normal(keys[0], -4.0, 4.0, (SEQS, LEN, HEADS), jnp.float32)
    location_list = jax.random.randint(keys[1], (SEQS, 4), 0, LEN)
    destination = jax.random.uniform(keys[2], (SEQS, 4), jnp.float32, 0.2, 0.5)
    segment_group = jnp.log(jnp.expm1(destination[:, :, None] / rate_entry)) - offset_bias_entry
    location_slot = lax.broadcasted_iota(jnp.int32, (SEQS, LEN, 1), 1)
    value_entries = noise
    for segment_group_index in range(4):
        matched_flag = location_slot == location_list[:, None, segment_group_index:segment_group_index + 1]
        value_entries = jnp.where(matched_flag, segment_group[:, segment_group_index][:, None, :], value_entries)
    return value_entries.astype(jnp.bfloat16)


def steps_of(own_key, shape, cuts, least, high):
    def one(dim, blocks):
        draws = jax.random.uniform(jax.random.fold_in(jax.random.fold_in(own_key, 6), dim), (blocks,), jnp.float32, least / len(cuts), high / len(cuts))
        return jnp.repeat(jnp.exp(draws), shape[dim] // blocks).reshape((-1,) + (1,) * (len(shape) - dim - 1))

    loudness = one(*cuts[0])
    for cut in cuts[1:]:
        loudness = loudness * one(*cut)
    return loudness


def normal_values(own_key, extent, scale, bound, pieces=(), kind=jnp.bfloat16):
    loudness = steps_of(own_key, extent, pieces, -0.22, 0.18) if pieces else 1.0
    values = jax.random.normal(own_key, extent, jnp.float32) * scale * loudness
    return jnp.minimum(jnp.maximum(values, -bound), bound).astype(kind)


def setup_inputs(seed: int = 0) -> dict:
    key_list = jax.random.split(jax.random.key(seed), 11)
    projected = normal_values(key_list[0], (SEQS, LEN, DI), 1.0, 6.0, ((1, 256),))
    state_maps = normal_values(key_list[1], (SEQS, LEN, 2 * GROUPS * STATE), 0.5, 3.0, ((1, 256),))
    step_raw = draw_step_raw(jax.random.fold_in(key_list[10], 71), 0)
    step_bias = draw_step_bias(jax.random.fold_in(key_list[10], 71), 0)
    decay_rate = draw_decay_rate(jax.random.fold_in(key_list[10], 71), 0)
    skip_gain = jnp.clip(0.5 + 1.0 * jax.random.uniform(key_list[5], (HEADS,), jnp.float32) ** steps_of(key_list[5], (HEADS,), ((0, 32),), -0.2, 0.2), 0.5, 1.5)
    conv_weight = normal_values(key_list[6], (CONV, DI), CONV ** -0.5, 3.0, ((1, 32),))
    conv_bias = normal_values(key_list[7], (DI,), 0.3, 1.5, ((0, 32),), jnp.float32)
    map_weight = normal_values(key_list[8], (CONV, 2 * GROUPS * STATE), CONV ** -0.5, 3.0)
    map_bias = normal_values(key_list[9], (2 * GROUPS * STATE,), 0.3, 1.5, (), jnp.float32)
    return dict(projected=projected, state_maps=state_maps, step_raw=step_raw, step_bias=step_bias, decay_rate=decay_rate, skip_gain=skip_gain, conv_weight=conv_weight, conv_bias=conv_bias, map_weight=map_weight, map_bias=map_bias)


def causal_conv(window, weight, bias, count):
    total = bias.astype(jnp.float32)
    for tap_index in range(CONV):
        part = lax.slice_in_dim(window, tap_index, tap_index + count, axis=0)
        total = total + weight[tap_index].astype(jnp.float32) * part.astype(jnp.float32)
    return jax.nn.silu(total).astype(jnp.bfloat16)


def one_sequence(projected, state_maps, step_raw, step_bias, decay_rate, skip_gain, conv_weight, conv_bias, map_weight, map_bias):
    width = HEADS * HEAD_DIM
    per_group = HEADS // GROUPS
    map_width = GROUPS * STATE
    padded_x = jnp.concatenate([jnp.zeros((CONV - 1, width), jnp.bfloat16), projected], axis=0)
    padded_maps = jnp.concatenate([jnp.zeros((CONV - 1, 2 * map_width), jnp.bfloat16), state_maps], axis=0)
    delta = jax.nn.softplus(step_raw.astype(jnp.float32) + step_bias)
    log_decay = -delta * decay_rate
    lower = jnp.arange(SPAN, dtype=jnp.int32)[:, None] >= jnp.arange(SPAN, dtype=jnp.int32)[None, :]

    def advance_span(state_in, index):
        offset = (index * SPAN).astype(jnp.int32)
        window_x = lax.dynamic_slice_in_dim(padded_x, offset, SPAN + CONV - 1, 0)
        window_maps = lax.dynamic_slice_in_dim(padded_maps, offset, SPAN + CONV - 1, 0)
        inner_x = causal_conv(window_x, conv_weight, conv_bias, SPAN).reshape(SPAN, HEADS, HEAD_DIM)
        inner_maps = causal_conv(window_maps, map_weight, map_bias, SPAN)
        inputs_b = inner_maps[:, :map_width].reshape(SPAN, GROUPS, STATE)
        outputs_c = inner_maps[:, map_width:].reshape(SPAN, GROUPS, STATE)
        delta_here = lax.dynamic_slice_in_dim(delta, offset, SPAN, 0)
        cumulative = jnp.cumsum(lax.dynamic_slice_in_dim(log_decay, offset, SPAN, 0), axis=0)
        scores = jnp.einsum("tgn,sgn->gts", outputs_c.astype(jnp.float32), inputs_b.astype(jnp.float32))
        scores = jnp.repeat(scores, per_group, axis=0)
        cum_heads = cumulative.T
        differ = cum_heads[:, :, None] - cum_heads[:, None, :]
        decay = jnp.where(lower, jnp.exp(jnp.minimum(differ, 0.0)), 0.0)
        weights = (scores * decay * delta_here.T[:, None, :]).astype(jnp.bfloat16)
        intra = jnp.einsum("hts,shp->thp", weights.astype(jnp.float32), inner_x.astype(jnp.float32))
        entering = state_in.astype(jnp.bfloat16).reshape(GROUPS, per_group, HEAD_DIM, STATE)
        inter = jnp.einsum("tgn,gjpn->tgjp", outputs_c.astype(jnp.float32), entering.astype(jnp.float32))
        inter = inter.reshape(SPAN, HEADS, HEAD_DIM)
        scale = jnp.exp(cumulative[-1:] - cumulative) * delta_here
        carried = (inner_x * scale[:, :, None]).astype(jnp.bfloat16).reshape(SPAN, GROUPS, per_group, HEAD_DIM)
        produced = jnp.einsum("sgjp,sgn->gjpn", carried.astype(jnp.float32), inputs_b.astype(jnp.float32))
        produced = produced.reshape(HEADS, HEAD_DIM, STATE)
        state_out = jnp.exp(cumulative[-1])[:, None, None] * state_in + produced
        mixed = intra + jnp.exp(cumulative)[:, :, None] * inter + skip_gain[None, :, None] * inner_x.astype(jnp.float32)
        return state_out, mixed.astype(jnp.bfloat16)

    start_state = jnp.zeros((HEADS, HEAD_DIM, STATE), jnp.float32)
    _, mixed = lax.scan(advance_span, start_state, jnp.arange(LEN // SPAN, dtype=jnp.int32))
    return mixed.reshape(LEN, width)


def reference(projected, state_maps, step_raw, step_bias, decay_rate, skip_gain, conv_weight, conv_bias, map_weight, map_bias):
    results = []
    for sequence in range(SEQS):
        results.append(one_sequence(projected[sequence], state_maps[sequence], step_raw[sequence], step_bias, decay_rate, skip_gain, conv_weight, conv_bias, map_weight, map_bias))
    return jnp.stack(results, axis=0)
```

```python
import jax
import jax.numpy as jnp
from jax import lax
from jax.experimental import pallas as pl
from jax.experimental.pallas import tpu as pltpu
from jax.sharding import PartitionSpec as P

MESH = pl.DeviceIdType.MESH
F32 = jnp.float32
BF16 = jnp.bfloat16
SPAN = 256
TOK = 64
LEN = 2048
SPANS = LEN // SPAN
NHEAD = 32
NSEQ = 8
BATCH = 4
CH = 256
EDGE = 16
DI = 16384
LOG2E = 1.4426950408889634
CAP = 64.0


def dot(a, b):
    return jnp.dot(a, b, preferred_element_type=F32)


def split(v):
    high = v.astype(BF16).astype(F32)
    rest = v - high
    middle = rest.astype(BF16).astype(F32)
    return high, middle, rest - middle


def silu(v):
    return v / (1.0 + jnp.exp(-v))


def kernel(
    proj, maps, step, sb, dr, sg, cw, cb, mw, mb, out,
    xin, mapin, mapc, bt, sc, xi, hs, hc, intra, ob, win, stt, stin, stf, pk, pkall,
    cumr, delr, work, rs, b2, zs1, zr1, zs2, hin, wrow,
    rx, rhx, rz1, rz2, rmap, rstep, rpar, rhm, rsib, rout,
    sx, smap, sstep, spar, shx, shm, ssib, sz1, sz2, sout,
):
    h = lax.axis_index("head")
    z = lax.axis_index("seq")
    g = h // 4
    r = lax.rem(h, 4)
    c = lax.rem(h, 2)
    seq = r // 2
    hb = g * 2 + c

    def peer(i):
        return lax.rem(h + i, NHEAD)

    def zpeer(i):
        return lax.rem(z + i, NSEQ)

    barrier = pltpu.get_barrier_semaphore()

    def greet(i, carry):
        pl.semaphore_signal(barrier, 1, device_id=(z, peer(i)), device_id_type=MESH)
        return carry

    def greet_z(i, carry):
        pl.semaphore_signal(barrier, 1, device_id=(zpeer(i), h), device_id_type=MESH)
        return carry

    lax.fori_loop(1, NHEAD, greet, 0)
    lax.fori_loop(1, NSEQ, greet_z, 0)
    pl.semaphore_wait(barrier, NHEAD - 1 + NSEQ - 1)

    def cols(start, width=CH):
        return pl.ds(pl.multiple_of(start, 128), width)

    def rows(start, count):
        return pl.ds(pl.multiple_of(start, 16), count)

    def map_src(d):
        return maps.at[lax.rem(d // 2, 2), :, cols(lax.rem(d, 2) * 2048 + (d // 4) * 256)]

    def x_src(d, b):
        base = ((d // 4) * 2 + lax.rem(d, 2)) * 1024
        return proj.at[lax.rem(d // 2, 2), :, cols(base + b * CH)]

    def st_src(d):
        return stt.at[lax.rem(d // 2, 2), rows(((d // 4) * 2 + lax.rem(d, 2)) * 16, 16), :]

    map_dst = mapin.at[rows(EDGE + h * TOK, TOK), :]

    def send_map(i, carry):
        d = peer(i)
        pltpu.make_async_remote_copy(
            map_src(d), map_dst, smap, rmap, device_id=(z, d), device_id_type=MESH
        ).start()
        return carry

    def send_x(b):
        dst = xin.at[b, rows(EDGE + h * TOK, TOK), :]
        pltpu.make_async_copy(x_src(h, b), dst, rx.at[b]).start()

        def one(i, carry):
            d = peer(i)
            pltpu.make_async_remote_copy(
                x_src(d, b), dst, sx, rx.at[b], device_id=(z, d), device_id_type=MESH
            ).start()
            return carry

        lax.fori_loop(1, NHEAD, one, 0)

    pltpu.make_async_copy(map_src(h), map_dst, rmap).start()
    lax.fori_loop(1, NHEAD, send_map, 0)
    send_x(0)

    eye = lax.broadcasted_iota(jnp.int32, (8, 8), 0) == lax.broadcasted_iota(jnp.int32, (8, 8), 1)

    def column(ref):
        return jnp.sum(jnp.where(eye, jnp.broadcast_to(ref[...], (8, 8)), 0.0), axis=1, keepdims=True)

    owner = lax.broadcasted_iota(jnp.int32, (8, 512), 1) // 64 == lax.broadcasted_iota(
        jnp.int32, (8, 512), 0
    )
    pk[0:4, 0:512] = cw[...].astype(F32)
    pk[4:5, 0:512] = cb[...]
    pk[5:6, 0:512] = jnp.sum(jnp.where(owner, column(sg), 0.0), axis=0, keepdims=True)
    pk[6:8, 0:512] = jnp.zeros((2, 512), F32)
    pk[:, 512:640] = jnp.broadcast_to(column(sb), (8, 128))
    pk[:, 640:768] = jnp.broadcast_to(column(dr), (8, 128))
    pltpu.make_async_copy(pk, pkall.at[r], rpar).start()
    for i in range(1, 4):
        pltpu.make_async_remote_copy(
            pk, pkall.at[r], spar, rpar, device_id=(z, g * 4 + lax.rem(r + i, 4)), device_id_type=MESH
        ).start()

    half = lax.broadcasted_iota(jnp.int32, (2 * TOK, 256), 0) // TOK == c
    for s in range(2):
        v = step[s].astype(F32)
        v = jnp.where(half, jnp.concatenate([v, v], axis=0), 0.0)
        stt[s] = v.T.astype(BF16)
    pltpu.make_async_copy(st_src(h), stin.at[h], rstep).start()

    def send_step(i, carry):
        d = peer(i)
        pltpu.make_async_remote_copy(
            st_src(d), stin.at[h], sstep, rstep, device_id=(z, d), device_id_type=MESH
        ).start()
        return carry

    lax.fori_loop(1, NHEAD, send_step, 0)
    send_x(1)

    def done(ref, sem):
        pltpu.make_async_copy(ref, ref, sem).wait()

    def conv(src, k, weight, bias, store):
        def part(i, carry):
            start = pl.multiple_of(k * SPAN + i * 64, 16)
            for j in range(2):
                lanes = slice(j * 128, (j + 1) * 128)
                win[j] = src[pl.ds(start, 64 + EDGE), lanes].astype(F32)
                total = bias[:, lanes]
                for tap in range(4):
                    total = total + weight[tap : tap + 1, lanes] * win[j, 13 + tap : 77 + tap, :]
                store(start, lanes, silu(total).astype(BF16))
            return carry

        lax.fori_loop(0, SPAN // 64, part, 0)

    def edge(buffer, send_sem, recv_sem):
        return pltpu.make_async_remote_copy(
            buffer.at[pl.ds(LEN, EDGE), :], buffer.at[pl.ds(0, EDGE), :],
            send_sem, recv_sem, device_id=(zpeer(1), h), device_id_type=MESH,
        )

    def first_block(buffer):
        @pl.when(z == 0)
        def _():
            buffer[0:EDGE, :] = jnp.zeros((EDGE, CH), BF16)

    done(pkall, rpar)
    done(stin, rstep)
    for i in range(16):
        stf[:, i * 128 : (i + 1) * 128] = stin[2 * i].astype(F32) + stin[2 * i + 1].astype(F32)
    bias_col = jnp.concatenate([pkall[2 * c, :, 512:513], pkall[2 * c + 1, :, 512:513]], axis=0)
    rate_col = jnp.concatenate([pkall[2 * c, :, 640:641], pkall[2 * c + 1, :, 640:641]], axis=0)
    upper = (
        lax.broadcasted_iota(jnp.int32, (SPAN, SPAN), 0)
        <= lax.broadcasted_iota(jnp.int32, (SPAN, SPAN), 1)
    ).astype(BF16)
    for k in range(SPANS):
        v = stf[:, k * SPAN : (k + 1) * SPAN] + bias_col
        delta = jnp.maximum(v, 0.0) + jnp.log1p(jnp.exp(-jnp.abs(v)))
        delr[k] = delta
        first, second, third = split(-delta * rate_col * LOG2E)
        cumr[k] = (
            dot(first.astype(BF16), upper) + dot(second.astype(BF16), upper)
        ) + dot(third.astype(BF16), upper)

    def rows_of(k, carry):
        cum = cumr[k]
        delta = delr[k]
        scale = jnp.exp2(cum[:, SPAN - 1 :] - cum) * delta
        s_high, s_low, _ = split(scale)
        e_high, e_mid, e_low = split(jnp.exp2(cum))
        work[0] = cum
        work[1] = s_high
        work[2] = s_low
        work[3] = e_high
        work[4] = e_mid
        work[5] = e_low
        work[6] = jnp.log(delta) * LOG2E - cum
        blank = jnp.zeros((4, SPAN), F32)
        for b in range(BATCH):
            at = slice(4 * b, 4 * b + 4)
            rs[k, b, 0:4] = work[0, at]
            rs[k, b, 4:8] = blank
            rs[k, b, 8:12] = work[1, at]
            rs[k, b, 12:16] = work[2, at]
            rs[k, b, 16:20] = work[3, at]
            rs[k, b, 20:24] = work[4, at]
            rs[k, b, 24:28] = work[5, at]
            rs[k, b, 28:32] = blank
            b2[k, b, 0:4] = work[6, at]
            b2[k, b, 4:8] = blank
        return carry

    lax.fori_loop(0, SPANS, rows_of, 0)
    send_x(2)

    done(mapin.at[pl.ds(EDGE, LEN), :], rmap)
    edge(mapin, shm, rhm).start()
    done(mapin.at[pl.ds(0, EDGE), :], rhm)
    first_block(mapin)
    which = cols(c * 2048 + g * 256)
    map_weight = mw[:, which].astype(F32)
    map_bias = mb[:, which]

    def map_span(k, carry):
        def store(start, lanes, value):
            mapc[c, pl.ds(start, 64), lanes] = value

        conv(mapin, k, map_weight, map_bias, store)
        return carry

    lax.fori_loop(0, SPANS, map_span, 0)
    pltpu.make_async_remote_copy(
        mapc.at[c], mapc.at[c], ssib, rsib, device_id=(z, g * 4 + seq * 2 + 1 - c), device_id_type=MESH
    ).start()
    done(mapc.at[1 - c], rsib)
    send_x(3)

    causal = lax.broadcasted_iota(jnp.int32, (SPAN, SPAN), 0) >= lax.broadcasted_iota(
        jnp.int32, (SPAN, SPAN), 1
    )

    def scores(k, carry):
        at = pl.ds(pl.multiple_of(k * SPAN, SPAN), SPAN)
        bt[k] = mapc[0, at, :].astype(F32).T.astype(BF16)
        sc[k] = jnp.where(causal, dot(mapc[1, at, :], bt[k]), 0.0)
        return carry

    lax.fori_loop(0, SPANS, scores, 0)

    row_id = lax.broadcasted_iota(jnp.int32, (32, CH), 0)
    same = lax.rem(row_id, 4) == lax.broadcasted_iota(jnp.int32, (32, CH), 1) // 64
    pick_scale = (same & (row_id >= 8) & (row_id < 16)).astype(BF16)
    pick_decay = (same & (row_id >= 16) & (row_id < 28)).astype(BF16)
    low_lanes = lax.broadcasted_iota(jnp.int32, (SPAN, 128), 1) < 64

    def params_of(b):
        return pkall.at[2 * c + b // 2, :, cols(lax.rem(b, 2) * CH)]

    def states(b):
        two = lax.rem(b, 2)
        done(xin.at[b, pl.ds(EDGE, LEN), :], rx.at[b])
        edge(xin.at[b], shx, rhx.at[b]).start()
        done(xin.at[b, pl.ds(0, EDGE), :], rhx.at[b])
        first_block(xin.at[b])
        par = params_of(b)
        weight = par[0:4, :]
        bias = par[4:5, :]
        hc[...] = jnp.zeros_like(hc)
        wrow[two, 0] = jnp.ones((8, CH), F32)

        def span(k, carry):
            def store(start, lanes, value):
                xi[two, pl.ds(start, 64), lanes] = value

            conv(xin.at[b], k, weight, bias, store)
            at = pl.ds(pl.multiple_of(k * SPAN, SPAN), SPAN)
            stack = rs[k, b].T.astype(BF16)
            scale = dot(stack, pick_scale)
            growth = dot(stack[SPAN - 16 :], pick_decay)[15:16]
            carried = (xi[two, at, :].astype(F32) * scale).astype(BF16)
            produced = dot(bt[k], carried)
            state = hc[...]
            hs[two, k] = state
            hc[...] = growth * state + produced
            wrow[two, k + 1] = wrow[two, k] * growth
            return carry

        lax.fori_loop(0, SPANS, span, 0)
        for j in range(NSEQ):
            zs1[b * NSEQ + j, 0:32, :] = hc[j * 32 : (j + 1) * 32, :]
            zs1[b * NSEQ + j, 32:40, :] = wrow[two, SPANS]
        pltpu.make_async_copy(zs1.at[b * NSEQ + z], zr1.at[b, z], rz1.at[b]).start()

        def send(i, carry):
            d = zpeer(i)
            pltpu.make_async_remote_copy(
                zs1.at[b * NSEQ + d], zr1.at[b, z], sz1, rz1.at[b], device_id=(d, h), device_id_type=MESH
            ).start()
            return carry

        lax.fori_loop(1, NSEQ, send, 0)

    def relay(b):
        done(zr1.at[b], rz1.at[b])
        state = jnp.zeros((32, CH), F32)
        for j in range(NSEQ):
            zs2[b * NSEQ + j] = state
            state = zr1[b, j, 32:33, :] * state + zr1[b, j, 0:32, :]
        here = hin.at[b, pl.ds(pl.multiple_of(z * 32, 32), 32), :]
        pltpu.make_async_copy(zs2.at[b * NSEQ + z], here, rz2.at[b]).start()

        def send(i, carry):
            d = zpeer(i)
            pltpu.make_async_remote_copy(
                zs2.at[b * NSEQ + d], here, sz2, rz2.at[b], device_id=(d, h), device_id_type=MESH
            ).start()
            return carry

        lax.fori_loop(1, NSEQ, send, 0)

    def within(b):
        two = lax.rem(b, 2)
        skip = params_of(b)[5:6, :]

        def span(k, carry):
            at = pl.ds(pl.multiple_of(k * SPAN, SPAN), SPAN)
            columns = rs[k, b, 0:8].T
            own = sc[k]
            for pair in range(2):
                lanes = slice(pair * 128, (pair + 1) * 128)
                x_pair = xi[two, at, lanes]
                sums = []
                for one in range(2):
                    i = pair * 2 + one
                    exponent = columns[:, i : i + 1] + b2[k, b, i : i + 1]
                    weights = (jnp.exp2(jnp.minimum(exponent, CAP)) * own).astype(BF16)
                    sums.append(dot(weights, x_pair))
                intra[two, at, lanes] = (
                    jnp.where(low_lanes, sums[0], sums[1]) + skip[:, lanes] * x_pair.astype(F32)
                )
            return carry

        lax.fori_loop(0, SPANS, span, 0)

    def finish(b):
        two = lax.rem(b, 2)
        done(hin.at[b], rz2.at[b])

        def span(i, carry):
            k = lax.rem(g + i, SPANS)
            at = pl.ds(pl.multiple_of(k * SPAN, SPAN), SPAN)
            entering = (hs[two, k] + wrow[two, k, 0:1] * hin[b]).astype(BF16)
            inter = dot(mapc[1, at, :], entering)
            decay = dot(rs[k, b].T.astype(BF16), pick_decay)
            ob[b, at, :] = (intra[two, at, :] + decay * inter).astype(BF16)
            for j in range(4):
                d = k * 4 + lax.rem(r + j, 4)
                src = ob.at[b, rows(d * TOK, TOK), :]
                dst = out.at[seq, :, cols(hb * 1024 + b * CH)]

                @pl.when(d == h)
                def _():
                    pltpu.make_async_copy(src, dst, rout).start()

                @pl.when(d != h)
                def _():
                    pltpu.make_async_remote_copy(
                        src, dst, sout, rout, device_id=(z, d), device_id_type=MESH
                    ).start()

            return carry

        lax.fori_loop(0, SPANS, span, 0)

    def turn(i, carry):
        @pl.when(i < BATCH)
        def _():
            states(i)

        @pl.when(i > 0)
        def _():
            relay(i - 1)

        @pl.when(i < BATCH)
        def _():
            within(i)

        @pl.when(i > 0)
        def _():
            finish(i - 1)

        return carry

    lax.fori_loop(0, BATCH + 1, turn, 0)

    most = DI - DI // NHEAD
    done(proj.at[:, :, pl.ds(0, most)], sx)
    done(mapin.at[pl.ds(0, LEN - TOK), :], smap)
    done(stin.at[pl.ds(0, NHEAD - 1)], sstep)
    done(pkall.at[pl.ds(0, 3)], spar)
    done(xin.at[0, pl.ds(0, BATCH * EDGE), :], shx)
    done(mapin.at[pl.ds(0, EDGE), :], shm)
    done(mapc.at[0], ssib)
    done(zs1.at[pl.ds(0, BATCH * (NSEQ - 1))], sz1)
    done(zs2.at[pl.ds(0, BATCH * (NSEQ - 1))], sz2)
    done(out.at[:, :, pl.ds(0, most)], sout)
    done(out, rout)


def local(proj, maps, step, sb, dr, sg, cw, cb, mw, mb):
    vmem = pl.BlockSpec(memory_space=pltpu.VMEM)
    hbm = pl.BlockSpec(memory_space=pl.ANY)
    dma = pltpu.SemaphoreType.DMA
    scratch = [
        pltpu.VMEM((BATCH, EDGE + LEN, CH), BF16),
        pltpu.VMEM((EDGE + LEN, CH), BF16),
        pltpu.VMEM((2, LEN, CH), BF16),
        pltpu.VMEM((SPANS, 256, SPAN), BF16),
        pltpu.VMEM((SPANS, SPAN, SPAN), F32),
        pltpu.VMEM((2, LEN, CH), BF16),
        pltpu.VMEM((2, SPANS, 256, CH), F32),
        pltpu.VMEM((256, CH), F32),
        pltpu.VMEM((2, LEN, CH), F32),
        pltpu.VMEM((BATCH, LEN, CH), BF16),
        pltpu.VMEM((2, 64 + EDGE, 128), F32),
        pltpu.VMEM((2, 256, 128), BF16),
        pltpu.VMEM((NHEAD, 16, 128), BF16),
        pltpu.VMEM((16, LEN), F32),
        pltpu.VMEM((8, 768), F32),
        pltpu.VMEM((4, 8, 768), F32),
        pltpu.VMEM((SPANS, 16, SPAN), F32),
        pltpu.VMEM((SPANS, 16, SPAN), F32),
        pltpu.VMEM((7, 16, SPAN), F32),
        pltpu.VMEM((SPANS, BATCH, 32, SPAN), F32),
        pltpu.VMEM((SPANS, BATCH, 8, SPAN), F32),
        pltpu.VMEM((BATCH * NSEQ, 40, CH), F32),
        pltpu.VMEM((BATCH, NSEQ, 40, CH), F32),
        pltpu.VMEM((BATCH * NSEQ, 32, CH), F32),
        pltpu.VMEM((BATCH, 256, CH), F32),
        pltpu.VMEM((2, SPANS + 1, 8, CH), F32),
    ]
    scratch += [dma((BATCH,))] * 4 + [dma] * 16
    return pl.pallas_call(
        kernel,
        out_shape=jax.ShapeDtypeStruct(proj.shape, BF16),
        in_specs=[hbm, hbm] + [vmem] * 8,
        out_specs=hbm,
        scratch_shapes=scratch,
        compiler_params=pltpu.CompilerParams(
            collective_id=0, has_side_effects=True, vmem_limit_bytes=48 * 1024 * 1024
        ),
    )(
        proj, maps, step, sb.reshape(1, -1), dr.reshape(1, -1), sg.reshape(1, -1),
        cw, cb.reshape(1, -1), mw, mb.reshape(1, -1),
    )


def solution(mesh):
    return jax.shard_map(
        local,
        mesh=mesh,
        in_specs=(
            P(None, ("seq", "head"), None),
            P(None, ("seq", "head"), None),
            P(None, ("seq", "head"), None),
            P("head"),
            P("head"),
            P("head"),
            P(None, "head"),
            P("head"),
            P(),
            P(),
        ),
        out_specs=P(None, ("seq", "head"), None),
        check_vma=False,
    )
```

```python
import jax
import jax.numpy as jnp
from jax import lax
from jax.experimental import pallas as pl
from jax.experimental.pallas import tpu as pltpu
from jax.sharding import PartitionSpec as P

MESH = pl.DeviceIdType.MESH
F32 = jnp.float32
BF16 = jnp.bfloat16
SPAN = 256
TOK = 64
LEN = 2048
SPANS = LEN // SPAN
NHEAD = 32
NSEQ = 8
BATCH = 4
CH = 256
STRIDE = 5
EDGE = 16
DI = 16384
LOG2E = 1.4426950408889634
CAP = 64.0


def dot(a, b):
    return jnp.dot(a, b, preferred_element_type=F32)


def split(v):
    high = v.astype(BF16).astype(F32)
    rest = v - high
    middle = rest.astype(BF16).astype(F32)
    return high, middle, rest - middle


def silu(v):
    return v / (1.0 + jnp.exp(-v))


def kernel(
    proj, maps, step_in, sb_in, dr_in, sg_in, cw_in, cb_in, mw_in, mb_in, out,
    step, sb, dr, sg, cw, cb, mw, mb,
    xin, mapin, mapc, bt, sc, xi, hs, intra, ob, win, stt, stin, stf, pk, pkall,
    cumr, delr, work, rs, b2, zs1, zr1, zs2, hin, wrow, grow,
    small, rx, rhx, rz1, rz2, rmap, rstep, rpar, rhm, rsib, rout,
    sx, smap, sstep, spar, shx, shm, ssib, sz1, sz2, sout,
):
    h = lax.axis_index("head")
    z = lax.axis_index("seq")
    g = h // 4
    r = lax.rem(h, 4)
    c = lax.rem(h, 2)
    seq = r // 2
    hb = g * 2 + c

    def peer(i):
        return lax.rem(h + i * STRIDE, NHEAD)

    def zpeer(i):
        return lax.rem(z + i, NSEQ)

    barrier = pltpu.get_barrier_semaphore()

    def greet(i, carry):
        pl.semaphore_signal(barrier, 1, device_id=(z, peer(i)), device_id_type=MESH)
        return carry

    def greet_z(i, carry):
        pl.semaphore_signal(barrier, 1, device_id=(zpeer(i), h), device_id_type=MESH)
        return carry

    lax.fori_loop(1, NHEAD, greet, 0)
    lax.fori_loop(1, NSEQ, greet_z, 0)
    arrivals = [
        pltpu.make_async_copy(src, dst, small.at[i])
        for i, (src, dst) in enumerate(
            [(step_in, step), (sb_in, sb), (dr_in, dr), (sg_in, sg), (cw_in, cw), (cb_in, cb),
             (mw_in, mw), (mb_in, mb)]
        )
    ]
    for arrival in arrivals:
        arrival.start()
    for arrival in arrivals:
        arrival.wait()

    def cols(start, width=CH):
        return pl.ds(pl.multiple_of(start, 128), width)

    def rows(start, count):
        return pl.ds(pl.multiple_of(start, 16), count)

    def map_src(d):
        return maps.at[lax.rem(d // 2, 2), :, cols(lax.rem(d, 2) * 2048 + (d // 4) * 256)]

    def x_src(d, b):
        base = ((d // 4) * 2 + lax.rem(d, 2)) * 1024
        return proj.at[lax.rem(d // 2, 2), :, cols(base + b * CH)]

    def st_src(d):
        return stt.at[lax.rem(d // 2, 2), rows(((d // 4) * 2 + lax.rem(d, 2)) * 16, 16), :]

    map_dst = mapin.at[rows(EDGE + h * TOK, TOK), :]

    def send_map(i, carry):
        d = peer(i)
        pltpu.make_async_remote_copy(
            map_src(d), map_dst, smap, rmap, device_id=(z, d), device_id_type=MESH
        ).start()
        return carry

    def send_x(b):
        dst = xin.at[b, rows(EDGE + h * TOK, TOK), :]
        pltpu.make_async_copy(x_src(h, b), dst, rx.at[b]).start()

        def one(i, carry):
            d = peer(i)
            pltpu.make_async_remote_copy(
                x_src(d, b), dst, sx, rx.at[b], device_id=(z, d), device_id_type=MESH
            ).start()
            return carry

        lax.fori_loop(1, NHEAD, one, 0)

    eye = lax.broadcasted_iota(jnp.int32, (8, 8), 0) == lax.broadcasted_iota(jnp.int32, (8, 8), 1)

    def column(ref):
        return jnp.sum(jnp.where(eye, jnp.broadcast_to(ref[...], (8, 8)), 0.0), axis=1, keepdims=True)

    owner = lax.broadcasted_iota(jnp.int32, (8, 512), 1) // 64 == lax.broadcasted_iota(
        jnp.int32, (8, 512), 0
    )
    pk[0:4, 0:512] = cw[...].astype(F32)
    pk[4:5, 0:512] = cb[...]
    pk[5:6, 0:512] = jnp.sum(jnp.where(owner, column(sg), 0.0), axis=0, keepdims=True)
    pk[6:8, 0:512] = jnp.zeros((2, 512), F32)
    pk[:, 512:640] = jnp.broadcast_to(column(sb), (8, 128))
    pk[:, 640:768] = jnp.broadcast_to(column(dr), (8, 128))

    half = lax.broadcasted_iota(jnp.int32, (2 * TOK, 256), 0) // TOK == c
    for s in range(2):
        v = step[s].astype(F32)
        v = jnp.where(half, jnp.concatenate([v, v], axis=0), 0.0)
        stt[s] = v.T.astype(BF16)

    def send_step(i, carry):
        d = peer(i)
        pltpu.make_async_remote_copy(
            st_src(d), stin.at[h], sstep, rstep, device_id=(z, d), device_id_type=MESH
        ).start()
        return carry

    pl.semaphore_wait(barrier, NHEAD - 1 + NSEQ - 1)
    pltpu.make_async_copy(pk, pkall.at[r], rpar).start()
    for i in range(1, 4):
        pltpu.make_async_remote_copy(
            pk, pkall.at[r], spar, rpar, device_id=(z, g * 4 + lax.rem(r + i, 4)), device_id_type=MESH
        ).start()
    pltpu.make_async_copy(st_src(h), stin.at[h], rstep).start()
    lax.fori_loop(1, NHEAD, send_step, 0)
    pltpu.make_async_copy(map_src(h), map_dst, rmap).start()
    lax.fori_loop(1, NHEAD, send_map, 0)
    for b in range(BATCH):
        send_x(b)

    def done(ref, sem):
        pltpu.make_async_copy(ref, ref, sem).wait()

    def conv(src, k, weight, bias, store):
        def part(i, carry):
            start = pl.multiple_of(k * SPAN + i * 64, 16)
            for j in range(2):
                lanes = slice(j * 128, (j + 1) * 128)
                win[j] = src[pl.ds(start, 64 + EDGE), lanes].astype(F32)
                total = bias[:, lanes]
                for tap in range(4):
                    total = total + weight[tap : tap + 1, lanes] * win[j, 13 + tap : 77 + tap, :]
                store(start, lanes, silu(total).astype(BF16))
            return carry

        lax.fori_loop(0, SPAN // 64, part, 0)

    def edge(buffer, send_sem, recv_sem):
        return pltpu.make_async_remote_copy(
            buffer.at[pl.ds(LEN, EDGE), :], buffer.at[pl.ds(0, EDGE), :],
            send_sem, recv_sem, device_id=(zpeer(1), h), device_id_type=MESH,
        )

    def first_block(buffer):
        @pl.when(z == 0)
        def _():
            buffer[0:EDGE, :] = jnp.zeros((EDGE, CH), BF16)

    done(pkall, rpar)
    done(stin, rstep)
    for i in range(16):
        stf[:, i * 128 : (i + 1) * 128] = stin[2 * i].astype(F32) + stin[2 * i + 1].astype(F32)
    bias_col = jnp.concatenate([pkall[2 * c, :, 512:513], pkall[2 * c + 1, :, 512:513]], axis=0)
    rate_col = jnp.concatenate([pkall[2 * c, :, 640:641], pkall[2 * c + 1, :, 640:641]], axis=0)
    upper = (
        lax.broadcasted_iota(jnp.int32, (SPAN, SPAN), 0)
        <= lax.broadcasted_iota(jnp.int32, (SPAN, SPAN), 1)
    ).astype(BF16)
    for k in range(SPANS):
        v = stf[:, k * SPAN : (k + 1) * SPAN] + bias_col
        delta = jnp.maximum(v, 0.0) + jnp.log1p(jnp.exp(-jnp.abs(v)))
        delr[k] = delta
        first, second, third = split(-delta * rate_col * LOG2E)
        cumr[k] = (
            dot(first.astype(BF16), upper) + dot(second.astype(BF16), upper)
        ) + dot(third.astype(BF16), upper)

    def rows_of(k, carry):
        cum = cumr[k]
        delta = delr[k]
        scale = jnp.exp2(cum[:, SPAN - 1 :] - cum) * delta
        s_high, s_low, _ = split(scale)
        e_high, e_mid, e_low = split(jnp.exp2(cum))
        work[0] = cum
        work[1] = s_high
        work[2] = s_low
        work[3] = e_high
        work[4] = e_mid
        work[5] = e_low
        work[6] = jnp.log(delta) * LOG2E - cum
        blank = jnp.zeros((4, SPAN), F32)
        for b in range(BATCH):
            at = slice(4 * b, 4 * b + 4)
            rs[k, b, 0:4] = work[0, at]
            rs[k, b, 4:8] = blank
            rs[k, b, 8:12] = work[1, at]
            rs[k, b, 12:16] = work[2, at]
            rs[k, b, 16:20] = work[3, at]
            rs[k, b, 20:24] = work[4, at]
            rs[k, b, 24:28] = work[5, at]
            rs[k, b, 28:32] = blank
            b2[k, b, 0:4] = work[6, at]
            b2[k, b, 4:8] = blank
        return carry

    lax.fori_loop(0, SPANS, rows_of, 0)

    done(mapin.at[pl.ds(EDGE, LEN), :], rmap)
    edge(mapin, shm, rhm).start()
    done(mapin.at[pl.ds(0, EDGE), :], rhm)
    first_block(mapin)
    which = cols(c * 2048 + g * 256)
    map_weight = mw[:, which].astype(F32)
    map_bias = mb[:, which]

    def map_span(k, carry):
        def store(start, lanes, value):
            mapc[c, pl.ds(start, 64), lanes] = value

        conv(mapin, k, map_weight, map_bias, store)
        return carry

    lax.fori_loop(0, SPANS, map_span, 0)
    sibling = pltpu.make_async_remote_copy(
        mapc.at[c], mapc.at[c], ssib, rsib, device_id=(z, g * 4 + seq * 2 + 1 - c), device_id_type=MESH
    )
    sibling.start()

    causal = lax.broadcasted_iota(jnp.int32, (SPAN, SPAN), 0) >= lax.broadcasted_iota(
        jnp.int32, (SPAN, SPAN), 1
    )

    def scores(k, carry):
        at = pl.ds(pl.multiple_of(k * SPAN, SPAN), SPAN)
        bt[k] = mapc[0, at, :].astype(F32).T.astype(BF16)
        sc[k] = jnp.where(causal, dot(mapc[1, at, :], bt[k]), 0.0)
        return carry


    row_id = lax.broadcasted_iota(jnp.int32, (32, CH), 0)
    same = lax.rem(row_id, 4) == lax.broadcasted_iota(jnp.int32, (32, CH), 1) // 64
    pick_scale = (same & (row_id >= 8) & (row_id < 16)).astype(BF16)
    pick_decay = (same & (row_id >= 16) & (row_id < 28)).astype(BF16)
    low_lanes = lax.broadcasted_iota(jnp.int32, (SPAN // 2, 128), 1) < 64

    def params_of(b):
        return pkall.at[2 * c + b // 2, :, cols(lax.rem(b, 2) * CH)]

    def convolve(b):
        two = lax.rem(b, 2)
        par = params_of(b)
        weight = par[0:4, :]
        bias = par[4:5, :]
        done(xin.at[b, pl.ds(EDGE, LEN), :], rx.at[b])
        edge(xin.at[b], shx, rhx.at[b]).start()

        def store(start, lanes, value):
            xi[two, pl.ds(start, 64), lanes] = value

        def span(k, carry):
            conv(xin.at[b], k, weight, bias, store)
            return carry

        lax.fori_loop(1, SPANS, span, 0)
        done(xin.at[b, pl.ds(0, EDGE), :], rhx.at[b])
        first_block(xin.at[b])
        span(0, 0)

    def states(b):
        two = lax.rem(b, 2)

        def produce(k):
            at = pl.ds(pl.multiple_of(k * SPAN, SPAN), SPAN)
            stack = rs[k, b].T.astype(BF16)
            scale = dot(stack, pick_scale)
            growth = dot(stack[SPAN - 16 :], pick_decay)[15:16]
            carried = (xi[two, at, :].astype(F32) * scale).astype(BF16)
            hs[two, k] = dot(bt[k], carried)
            grow[k] = jnp.broadcast_to(growth, (8, CH))

        def spans(i, carry):
            produce(2 * i)
            produce(2 * i + 1)
            return carry

        lax.fori_loop(0, SPANS // 2, spans, 0)
        total = jnp.ones((8, CH), F32)
        for k in range(SPANS):
            wrow[two, k] = total
            total = total * grow[k]
        first, second, third = split(total[0:1])
        line = lax.broadcasted_iota(jnp.int32, (16, CH), 0)
        growth_rows = jnp.where(
            line == 0, first, jnp.where(line == 1, second, jnp.where(line == 2, third, 0.0))
        ).astype(BF16)

        def scan(j, carry):
            part = pl.ds(pl.multiple_of(j * 32, 32), 32)
            state = jnp.zeros((32, CH), F32)
            for k in range(SPANS):
                made = hs[two, k, part, :]
                hs[two, k, part, :] = state
                state = grow[k, 0:1] * state + made
            zs1[b * NSEQ + j, 0:32, :] = state.astype(BF16)
            zs1[b * NSEQ + j, 32:48, :] = growth_rows
            return carry

        lax.fori_loop(0, NSEQ, scan, 0)
        pltpu.make_async_copy(zs1.at[b * NSEQ + z], zr1.at[b, z], rz1.at[b]).start()

        def send(i, carry):
            d = zpeer(i)
            pltpu.make_async_remote_copy(
                zs1.at[b * NSEQ + d], zr1.at[b, z], sz1, rz1.at[b], device_id=(d, h), device_id_type=MESH
            ).start()
            return carry

        lax.fori_loop(1, NSEQ, send, 0)

    def relay(b):
        done(zr1.at[b], rz1.at[b])
        state = jnp.zeros((32, CH), F32)
        for j in range(NSEQ):
            zs2[b * NSEQ + j] = state.astype(BF16)
            growth = zr1[b, j, 32:48, :].astype(F32)
            growth = growth[0:1] + growth[1:2] + growth[2:3]
            state = growth * state + zr1[b, j, 0:32, :].astype(F32)
        here = hin.at[b, pl.ds(pl.multiple_of(z * 32, 32), 32), :]
        pltpu.make_async_copy(zs2.at[b * NSEQ + z], here, rz2.at[b]).start()

        def send(i, carry):
            d = zpeer(i)
            pltpu.make_async_remote_copy(
                zs2.at[b * NSEQ + d], here, sz2, rz2.at[b], device_id=(d, h), device_id_type=MESH
            ).start()
            return carry

        lax.fori_loop(1, NSEQ, send, 0)

    HALF = SPAN // 2

    def within(b):
        two = lax.rem(b, 2)
        skip = params_of(b)[5:6, :]

        def one_span(k):
            columns = rs[k, b, 0:8].T
            for pair in range(2):
                lanes = slice(pair * 128, (pair + 1) * 128)
                at = pl.ds(pl.multiple_of(k * SPAN, SPAN), SPAN)
                x_pair = xi[two, at, lanes]
                early = []
                late = []
                for one in range(2):
                    i = pair * 2 + one
                    row = b2[k, b, i : i + 1]
                    a_early = columns[:HALF, i : i + 1]
                    a_late = columns[HALF:, i : i + 1]
                    w = jnp.exp2(jnp.minimum(a_early + row[:, :HALF], CAP)) * sc[k, :HALF, :HALF]
                    early.append(dot(w.astype(BF16), x_pair[:HALF]))
                    w_old = jnp.exp2(a_late + row[:, :HALF]) * sc[k, HALF:, :HALF]
                    w_own = jnp.exp2(jnp.minimum(a_late + row[:, HALF:], CAP)) * sc[k, HALF:, HALF:]
                    w = jnp.concatenate([w_old.astype(BF16), w_own.astype(BF16)], axis=1)
                    late.append(dot(w, x_pair))
                direct = skip[:, lanes] * x_pair.astype(F32)
                start = pl.multiple_of(k * SPAN, SPAN)
                intra[two, pl.ds(start, HALF), lanes] = (
                    jnp.where(low_lanes, early[0], early[1]) + direct[:HALF]
                )
                intra[two, pl.ds(start + HALF, HALF), lanes] = (
                    jnp.where(low_lanes, late[0], late[1]) + direct[HALF:]
                )

        def spans(i, carry):
            one_span(2 * i)
            one_span(2 * i + 1)
            return carry

        lax.fori_loop(0, SPANS // 2, spans, 0)

    def finish(b):
        two = lax.rem(b, 2)
        done(hin.at[b], rz2.at[b])

        def span(k):
            at = pl.ds(pl.multiple_of(k * SPAN, SPAN), SPAN)
            entering = (hs[two, k] + wrow[two, k, 0:1] * hin[b].astype(F32)).astype(BF16)
            inter = dot(mapc[1, at, :], entering)
            decay = dot(rs[k, b].T.astype(BF16), pick_decay)
            ob[b, at, :] = (intra[two, at, :] + decay * inter).astype(BF16)

        def spans(i, carry):
            span(2 * i)
            span(2 * i + 1)
            return carry

        lax.fori_loop(0, SPANS // 2, spans, 0)
        dst = out.at[seq, :, cols(hb * 1024 + b * CH)]

        def leave(i, carry):
            d = peer(i)
            pltpu.make_async_remote_copy(
                ob.at[b, rows(d * TOK, TOK), :], dst, sout, rout, device_id=(z, d), device_id_type=MESH
            ).start()
            return carry

        pltpu.make_async_copy(ob.at[b, rows(h * TOK, TOK), :], dst, rout).start()
        lax.fori_loop(1, NHEAD, leave, 0)

    def turn(i, carry):
        @pl.when(i > 0)
        def _():
            relay(i - 1)

        @pl.when(i < BATCH)
        def _():
            convolve(i)

        @pl.when(i == 0)
        def _():
            done(mapc.at[1 - c], rsib)
            lax.fori_loop(0, SPANS, scores, 0)

        @pl.when(i < BATCH)
        def _():
            states(i)

        @pl.when(i > 0)
        def _():
            finish(i - 1)

        @pl.when(i < BATCH)
        def _():
            within(i)

        return carry

    lax.fori_loop(0, BATCH + 1, turn, 0)

    most = DI - DI // NHEAD
    done(proj.at[:, :, pl.ds(0, most)], sx)
    done(mapin.at[pl.ds(0, LEN - TOK), :], smap)
    done(stin.at[pl.ds(0, NHEAD - 1)], sstep)
    done(pkall.at[pl.ds(0, 3)], spar)
    done(xin.at[0, pl.ds(0, BATCH * EDGE), :], shx)
    done(mapin.at[pl.ds(0, EDGE), :], shm)
    done(mapc.at[0], ssib)
    done(zs1.at[pl.ds(0, BATCH * (NSEQ - 1))], sz1)
    done(zs2.at[pl.ds(0, BATCH * (NSEQ - 1))], sz2)
    done(out.at[:, :, pl.ds(0, most)], sout)
    done(out, rout)


def local(proj, maps, step, sb, dr, sg, cw, cb, mw, mb):
    hbm = pl.BlockSpec(memory_space=pltpu.HBM)
    dma = pltpu.SemaphoreType.DMA
    scratch = [
        pltpu.VMEM(step.shape, BF16),
        pltpu.VMEM((1, 8), F32),
        pltpu.VMEM((1, 8), F32),
        pltpu.VMEM((1, 8), F32),
        pltpu.VMEM(cw.shape, BF16),
        pltpu.VMEM((1, 512), F32),
        pltpu.VMEM(mw.shape, BF16),
        pltpu.VMEM((1, 4096), F32),
        pltpu.VMEM((BATCH, EDGE + LEN, CH), BF16),
        pltpu.VMEM((EDGE + LEN, CH), BF16),
        pltpu.VMEM((2, LEN, CH), BF16),
        pltpu.VMEM((SPANS, 256, SPAN), BF16),
        pltpu.VMEM((SPANS, SPAN, SPAN), F32),
        pltpu.VMEM((2, LEN, CH), BF16),
        pltpu.VMEM((2, SPANS, 256, CH), F32),
        pltpu.VMEM((2, LEN, CH), F32),
        pltpu.VMEM((BATCH, LEN, CH), BF16),
        pltpu.VMEM((2, 64 + EDGE, 128), F32),
        pltpu.VMEM((2, 256, 128), BF16),
        pltpu.VMEM((NHEAD, 16, 128), BF16),
        pltpu.VMEM((16, LEN), F32),
        pltpu.VMEM((8, 768), F32),
        pltpu.VMEM((4, 8, 768), F32),
        pltpu.VMEM((SPANS, 16, SPAN), F32),
        pltpu.VMEM((SPANS, 16, SPAN), F32),
        pltpu.VMEM((7, 16, SPAN), F32),
        pltpu.VMEM((SPANS, BATCH, 32, SPAN), F32),
        pltpu.VMEM((SPANS, BATCH, 8, SPAN), F32),
        pltpu.VMEM((BATCH * NSEQ, 48, CH), BF16),
        pltpu.VMEM((BATCH, NSEQ, 48, CH), BF16),
        pltpu.VMEM((BATCH * NSEQ, 32, CH), BF16),
        pltpu.VMEM((BATCH, 256, CH), BF16),
        pltpu.VMEM((2, SPANS, 8, CH), F32),
        pltpu.VMEM((SPANS, 8, CH), F32),
    ]
    scratch += [dma((8,))] + [dma((BATCH,))] * 4 + [dma] * 16
    return pl.pallas_call(
        kernel,
        out_shape=jax.ShapeDtypeStruct(proj.shape, BF16),
        in_specs=[hbm] * 10,
        out_specs=pl.BlockSpec(memory_space=pl.ANY),
        scratch_shapes=scratch,
        compiler_params=pltpu.CompilerParams(
            collective_id=0, has_side_effects=True, vmem_limit_bytes=62 * 1024 * 1024
        ),
    )(
        proj, maps, step, sb.reshape(1, -1), dr.reshape(1, -1), sg.reshape(1, -1),
        cw, cb.reshape(1, -1), mw, mb.reshape(1, -1),
    )


def solution(mesh):
    return jax.shard_map(
        local,
        mesh=mesh,
        in_specs=(
            P(None, ("seq", "head"), None),
            P(None, ("seq", "head"), None),
            P(None, ("seq", "head"), None),
            P("head"),
            P("head"),
            P("head"),
            P(None, "head"),
            P("head"),
            P(),
            P(),
        ),
        out_specs=P(None, ("seq", "head"), None),
        check_vma=False,
    )
```

```python
import jax
import jax.numpy as jnp
from jax import lax
from jax.experimental import pallas as pl
from jax.experimental.pallas import tpu as pltpu
from jax.sharding import PartitionSpec as P

MESH = pl.DeviceIdType.MESH
F32 = jnp.float32
BF16 = jnp.bfloat16
SPAN = 256
TOK = 64
LEN = 2048
SPANS = LEN // SPAN
NHEAD = 32
NSEQ = 8
BATCH = 4
CH = 256
STRIDE = 5
EDGE = 16
DI = 16384
LOG2E = 1.4426950408889634
CAP = 64.0


def dot(a, b):
    return jnp.dot(a, b, preferred_element_type=F32)


def split(v):
    high = v.astype(BF16).astype(F32)
    rest = v - high
    middle = rest.astype(BF16).astype(F32)
    return high, middle, rest - middle


def silu(v):
    return v / (1.0 + jnp.exp(-v))


def kernel(
    proj, maps, step_in, sb_in, dr_in, sg_in, cw_in, cb_in, mw_in, mb_in, out,
    step, sb, dr, sg, cw, cb, mw, mb,
    xin, mapin, mapc, bt, sc, xi, hs, intra, ob, win, stt, stin, stf, pk, pkall,
    cumr, delr, work, rs, b2, zs1, zr1, zs2, hin, wrow, grow,
    small, rx, rhx, rz1, rz2, rmap, rstep, rpar, rhm, rsib, rout,
    sx, smap, sstep, spar, shx, shm, ssib, sz1, sz2, sout,
):
    h = lax.axis_index("head")
    z = lax.axis_index("seq")
    g = h // 4
    r = lax.rem(h, 4)
    c = lax.rem(h, 2)
    seq = r // 2
    hb = g * 2 + c

    def peer(i):
        return lax.rem(h + i * STRIDE, NHEAD)

    def zpeer(i):
        return lax.rem(z + i, NSEQ)

    barrier = pltpu.get_barrier_semaphore()

    def greet(i, carry):
        pl.semaphore_signal(barrier, 1, device_id=(z, peer(i)), device_id_type=MESH)
        return carry

    def greet_z(i, carry):
        pl.semaphore_signal(barrier, 1, device_id=(zpeer(i), h), device_id_type=MESH)
        return carry

    lax.fori_loop(1, NHEAD, greet, 0)
    lax.fori_loop(1, NSEQ, greet_z, 0)
    arrivals = [
        pltpu.make_async_copy(src, dst, small.at[i])
        for i, (src, dst) in enumerate(
            [(step_in, step), (sb_in, sb), (dr_in, dr), (sg_in, sg), (cw_in, cw), (cb_in, cb),
             (mw_in, mw), (mb_in, mb)]
        )
    ]
    for arrival in arrivals:
        arrival.start()
    for arrival in arrivals:
        arrival.wait()

    def cols(start, width=CH):
        return pl.ds(pl.multiple_of(start, 128), width)

    def rows(start, count):
        return pl.ds(pl.multiple_of(start, 16), count)

    def map_src(d):
        return maps.at[lax.rem(d // 2, 2), :, cols(lax.rem(d, 2) * 2048 + (d // 4) * 256)]

    def x_src(d, b):
        base = ((d // 4) * 2 + lax.rem(d, 2)) * 1024
        return proj.at[lax.rem(d // 2, 2), :, cols(base + b * CH)]

    def st_src(d):
        return stt.at[lax.rem(d // 2, 2), rows(((d // 4) * 2 + lax.rem(d, 2)) * 16, 16), :]

    map_dst = mapin.at[rows(EDGE + h * TOK, TOK), :]

    def send_map(i, carry):
        d = peer(i)
        pltpu.make_async_remote_copy(
            map_src(d), map_dst, smap, rmap, device_id=(z, d), device_id_type=MESH
        ).start()
        return carry

    def send_x(b):
        dst = xin.at[b, rows(EDGE + h * TOK, TOK), :]
        pltpu.make_async_copy(x_src(h, b), dst, rx.at[b]).start()

        def one(i, carry):
            d = peer(i)
            pltpu.make_async_remote_copy(
                x_src(d, b), dst, sx, rx.at[b], device_id=(z, d), device_id_type=MESH
            ).start()
            return carry

        lax.fori_loop(1, NHEAD, one, 0)

    eye = lax.broadcasted_iota(jnp.int32, (8, 8), 0) == lax.broadcasted_iota(jnp.int32, (8, 8), 1)

    def column(ref):
        return jnp.sum(jnp.where(eye, jnp.broadcast_to(ref[...], (8, 8)), 0.0), axis=1, keepdims=True)

    owner = lax.broadcasted_iota(jnp.int32, (8, 512), 1) // 64 == lax.broadcasted_iota(
        jnp.int32, (8, 512), 0
    )
    pk[0:4, 0:512] = cw[...].astype(F32)
    pk[4:5, 0:512] = cb[...]
    pk[5:6, 0:512] = jnp.sum(jnp.where(owner, column(sg), 0.0), axis=0, keepdims=True)
    pk[6:8, 0:512] = jnp.zeros((2, 512), F32)
    pk[:, 512:640] = jnp.broadcast_to(column(sb), (8, 128))
    pk[:, 640:768] = jnp.broadcast_to(column(dr), (8, 128))

    half = lax.broadcasted_iota(jnp.int32, (2 * TOK, 256), 0) // TOK == c
    for s in range(2):
        v = step[s].astype(F32)
        v = jnp.where(half, jnp.concatenate([v, v], axis=0), 0.0)
        stt[s] = v.T.astype(BF16)

    def send_step(i, carry):
        d = peer(i)
        pltpu.make_async_remote_copy(
            st_src(d), stin.at[h], sstep, rstep, device_id=(z, d), device_id_type=MESH
        ).start()
        return carry

    pl.semaphore_wait(barrier, NHEAD - 1 + NSEQ - 1)
    pltpu.make_async_copy(pk, pkall.at[r], rpar).start()
    for i in range(1, 4):
        pltpu.make_async_remote_copy(
            pk, pkall.at[r], spar, rpar, device_id=(z, g * 4 + lax.rem(r + i, 4)), device_id_type=MESH
        ).start()
    pltpu.make_async_copy(st_src(h), stin.at[h], rstep).start()
    lax.fori_loop(1, NHEAD, send_step, 0)
    pltpu.make_async_copy(map_src(h), map_dst, rmap).start()
    lax.fori_loop(1, NHEAD, send_map, 0)
    for b in range(BATCH):
        send_x(b)

    def done(ref, sem):
        pltpu.make_async_copy(ref, ref, sem).wait()

    def conv(src, k, weight, bias, store):
        def part(i, carry):
            start = pl.multiple_of(k * SPAN + i * 64, 16)
            for j in range(2):
                lanes = slice(j * 128, (j + 1) * 128)
                win[j] = src[pl.ds(start, 64 + EDGE), lanes].astype(F32)
                total = bias[:, lanes]
                for tap in range(4):
                    total = total + weight[tap : tap + 1, lanes] * win[j, 13 + tap : 77 + tap, :]
                store(start, lanes, silu(total).astype(BF16))
            return carry

        lax.fori_loop(0, SPAN // 64, part, 0)

    def edge(buffer, send_sem, recv_sem):
        return pltpu.make_async_remote_copy(
            buffer.at[pl.ds(LEN, EDGE), :], buffer.at[pl.ds(0, EDGE), :],
            send_sem, recv_sem, device_id=(zpeer(1), h), device_id_type=MESH,
        )

    def first_block(buffer):
        @pl.when(z == 0)
        def _():
            buffer[0:EDGE, :] = jnp.zeros((EDGE, CH), BF16)

    done(pkall, rpar)
    done(stin, rstep)
    for i in range(16):
        stf[:, i * 128 : (i + 1) * 128] = stin[2 * i].astype(F32) + stin[2 * i + 1].astype(F32)
    bias_col = jnp.concatenate([pkall[2 * c, :, 512:513], pkall[2 * c + 1, :, 512:513]], axis=0)
    rate_col = jnp.concatenate([pkall[2 * c, :, 640:641], pkall[2 * c + 1, :, 640:641]], axis=0)
    upper = (
        lax.broadcasted_iota(jnp.int32, (SPAN, SPAN), 0)
        <= lax.broadcasted_iota(jnp.int32, (SPAN, SPAN), 1)
    ).astype(BF16)
    for k in range(SPANS):
        v = stf[:, k * SPAN : (k + 1) * SPAN] + bias_col
        delta = jnp.maximum(v, 0.0) + jnp.log1p(jnp.exp(-jnp.abs(v)))
        delr[k] = delta
        first, second, third = split(-delta * rate_col * LOG2E)
        cumr[k] = (
            dot(first.astype(BF16), upper) + dot(second.astype(BF16), upper)
        ) + dot(third.astype(BF16), upper)

    def rows_of(k, carry):
        cum = cumr[k]
        delta = delr[k]
        scale = jnp.exp2(cum[:, SPAN - 1 :] - cum) * delta
        s_high, s_low, _ = split(scale)
        e_high, e_mid, e_low = split(jnp.exp2(cum))
        work[0] = cum
        work[1] = s_high
        work[2] = s_low
        work[3] = e_high
        work[4] = e_mid
        work[5] = e_low
        work[6] = jnp.log(delta) * LOG2E - cum
        blank = jnp.zeros((4, SPAN), F32)
        for b in range(BATCH):
            at = slice(4 * b, 4 * b + 4)
            rs[k, b, 0:4] = work[0, at]
            rs[k, b, 4:8] = blank
            rs[k, b, 8:12] = work[1, at]
            rs[k, b, 12:16] = work[2, at]
            rs[k, b, 16:20] = work[3, at]
            rs[k, b, 20:24] = work[4, at]
            rs[k, b, 24:28] = work[5, at]
            rs[k, b, 28:32] = blank
            b2[k, b, 0:4] = work[6, at]
            b2[k, b, 4:8] = blank
        return carry

    lax.fori_loop(0, SPANS, rows_of, 0)

    done(mapin.at[pl.ds(EDGE, LEN), :], rmap)
    edge(mapin, shm, rhm).start()
    done(mapin.at[pl.ds(0, EDGE), :], rhm)
    first_block(mapin)
    which = cols(c * 2048 + g * 256)
    map_weight = mw[:, which].astype(F32)
    map_bias = mb[:, which]

    def map_span(k, carry):
        def store(start, lanes, value):
            mapc[c, pl.ds(start, 64), lanes] = value

        conv(mapin, k, map_weight, map_bias, store)
        return carry

    lax.fori_loop(0, SPANS, map_span, 0)
    sibling = pltpu.make_async_remote_copy(
        mapc.at[c], mapc.at[c], ssib, rsib, device_id=(z, g * 4 + seq * 2 + 1 - c), device_id_type=MESH
    )
    sibling.start()

    causal = lax.broadcasted_iota(jnp.int32, (SPAN, SPAN), 0) >= lax.broadcasted_iota(
        jnp.int32, (SPAN, SPAN), 1
    )

    def scores(k, carry):
        at = pl.ds(pl.multiple_of(k * SPAN, SPAN), SPAN)
        bt[k] = mapc[0, at, :].astype(F32).T.astype(BF16)
        sc[k] = jnp.where(causal, dot(mapc[1, at, :], bt[k]), 0.0)
        return carry


    row_id = lax.broadcasted_iota(jnp.int32, (32, CH), 0)
    same = lax.rem(row_id, 4) == lax.broadcasted_iota(jnp.int32, (32, CH), 1) // 64
    pick_scale = (same & (row_id >= 8) & (row_id < 16)).astype(BF16)
    pick_decay = (same & (row_id >= 16) & (row_id < 28)).astype(BF16)
    low_lanes = lax.broadcasted_iota(jnp.int32, (SPAN // 2, 128), 1) < 64

    def params_of(b):
        return pkall.at[2 * c + b // 2, :, cols(lax.rem(b, 2) * CH)]

    def convolve(b):
        two = lax.rem(b, 2)
        par = params_of(b)
        weight = par[0:4, :]
        bias = par[4:5, :]
        done(xin.at[b, pl.ds(EDGE, LEN), :], rx.at[b])
        edge(xin.at[b], shx, rhx.at[b]).start()

        def store(start, lanes, value):
            xi[two, pl.ds(start, 64), lanes] = value

        def span(k, carry):
            conv(xin.at[b], k, weight, bias, store)
            return carry

        lax.fori_loop(1, SPANS, span, 0)
        done(xin.at[b, pl.ds(0, EDGE), :], rhx.at[b])
        first_block(xin.at[b])
        span(0, 0)

    def states(b):
        two = lax.rem(b, 2)

        def produce(k):
            at = pl.ds(pl.multiple_of(k * SPAN, SPAN), SPAN)
            stack = rs[k, b].T.astype(BF16)
            scale = dot(stack, pick_scale)
            growth = dot(stack[SPAN - 16 :], pick_decay)[15:16]
            carried = (xi[two, at, :].astype(F32) * scale).astype(BF16)
            hs[two, k] = dot(bt[k], carried)
            grow[k] = jnp.broadcast_to(growth, (8, CH))

        def spans(i, carry):
            produce(2 * i)
            produce(2 * i + 1)
            return carry

        lax.fori_loop(0, SPANS // 2, spans, 0)
        total = jnp.ones((8, CH), F32)
        for k in range(SPANS):
            wrow[two, k] = total
            total = total * grow[k]
        first, second, third = split(total[0:1])
        line = lax.broadcasted_iota(jnp.int32, (16, CH), 0)
        growth_rows = jnp.where(
            line == 0, first, jnp.where(line == 1, second, jnp.where(line == 2, third, 0.0))
        ).astype(BF16)

        def scan(j, carry):
            part = pl.ds(pl.multiple_of(j * 32, 32), 32)
            state = jnp.zeros((32, CH), F32)
            for k in range(SPANS):
                made = hs[two, k, part, :]
                hs[two, k, part, :] = state
                state = grow[k, 0:1] * state + made
            zs1[b * NSEQ + j, 0:32, :] = state.astype(BF16)
            zs1[b * NSEQ + j, 32:48, :] = growth_rows
            return carry

        lax.fori_loop(0, NSEQ, scan, 0)
        pltpu.make_async_copy(zs1.at[b * NSEQ + z], zr1.at[b, z], rz1.at[b]).start()

        def send(i, carry):
            d = zpeer(i)
            pltpu.make_async_remote_copy(
                zs1.at[b * NSEQ + d], zr1.at[b, z], sz1, rz1.at[b], device_id=(d, h), device_id_type=MESH
            ).start()
            return carry

        lax.fori_loop(1, NSEQ, send, 0)

    def relay(b):
        done(zr1.at[b], rz1.at[b])
        state = jnp.zeros((32, CH), F32)
        for j in range(NSEQ):
            zs2[b * NSEQ + j] = state.astype(BF16)
            growth = zr1[b, j, 32:48, :].astype(F32)
            growth = growth[0:1] + growth[1:2] + growth[2:3]
            state = growth * state + zr1[b, j, 0:32, :].astype(F32)
        here = hin.at[b, pl.ds(pl.multiple_of(z * 32, 32), 32), :]
        pltpu.make_async_copy(zs2.at[b * NSEQ + z], here, rz2.at[b]).start()

        def send(i, carry):
            d = zpeer(i)
            pltpu.make_async_remote_copy(
                zs2.at[b * NSEQ + d], here, sz2, rz2.at[b], device_id=(d, h), device_id_type=MESH
            ).start()
            return carry

        lax.fori_loop(1, NSEQ, send, 0)

    HALF = SPAN // 2

    def within(b):
        two = lax.rem(b, 2)
        skip = params_of(b)[5:6, :]

        def one_span(k):
            columns = rs[k, b, 0:8].T
            for pair in range(2):
                lanes = slice(pair * 128, (pair + 1) * 128)
                at = pl.ds(pl.multiple_of(k * SPAN, SPAN), SPAN)
                x_pair = xi[two, at, lanes]
                early = []
                late = []
                for one in range(2):
                    i = pair * 2 + one
                    row = b2[k, b, i : i + 1]
                    a_early = columns[:HALF, i : i + 1]
                    a_late = columns[HALF:, i : i + 1]
                    w = jnp.exp2(jnp.minimum(a_early + row[:, :HALF], CAP)) * sc[k, :HALF, :HALF]
                    early.append(dot(w.astype(BF16), x_pair[:HALF]))
                    w_old = jnp.exp2(a_late + row[:, :HALF]) * sc[k, HALF:, :HALF]
                    w_own = jnp.exp2(jnp.minimum(a_late + row[:, HALF:], CAP)) * sc[k, HALF:, HALF:]
                    w = jnp.concatenate([w_old.astype(BF16), w_own.astype(BF16)], axis=1)
                    late.append(dot(w, x_pair))
                direct = skip[:, lanes] * x_pair.astype(F32)
                start = pl.multiple_of(k * SPAN, SPAN)
                intra[two, pl.ds(start, HALF), lanes] = (
                    jnp.where(low_lanes, early[0], early[1]) + direct[:HALF]
                )
                intra[two, pl.ds(start + HALF, HALF), lanes] = (
                    jnp.where(low_lanes, late[0], late[1]) + direct[HALF:]
                )

        def spans(i, carry):
            one_span(2 * i)
            one_span(2 * i + 1)
            return carry

        lax.fori_loop(0, SPANS // 2, spans, 0)

    def finish(b):
        two = lax.rem(b, 2)
        done(hin.at[b], rz2.at[b])

        def span(k):
            at = pl.ds(pl.multiple_of(k * SPAN, SPAN), SPAN)
            entering = (hs[two, k] + wrow[two, k, 0:1] * hin[b].astype(F32)).astype(BF16)
            inter = dot(mapc[1, at, :], entering)
            decay = dot(rs[k, b].T.astype(BF16), pick_decay)
            ob[b, at, :] = (intra[two, at, :] + decay * inter).astype(BF16)

        def spans(i, carry):
            span(2 * i)
            span(2 * i + 1)
            return carry

        lax.fori_loop(0, SPANS // 2, spans, 0)
        dst = out.at[seq, :, cols(hb * 1024 + b * CH)]

        def leave(i, carry):
            d = peer(i)
            pltpu.make_async_remote_copy(
                ob.at[b, rows(d * TOK, TOK), :], dst, sout, rout, device_id=(z, d), device_id_type=MESH
            ).start()
            return carry

        pltpu.make_async_copy(ob.at[b, rows(h * TOK, TOK), :], dst, rout).start()
        lax.fori_loop(1, NHEAD, leave, 0)

    def turn(i, carry):
        @pl.when(i > 0)
        def _():
            relay(i - 1)

        @pl.when(i < BATCH)
        def _():
            convolve(i)

        @pl.when(i == 0)
        def _():
            done(mapc.at[1 - c], rsib)
            lax.fori_loop(0, SPANS, scores, 0)

        @pl.when(i < BATCH)
        def _():
            states(i)

        @pl.when(i > 0)
        def _():
            finish(i - 1)

        @pl.when(i < BATCH)
        def _():
            within(i)

        return carry

    lax.fori_loop(0, BATCH + 1, turn, 0)

    most = DI - DI // NHEAD
    done(proj.at[:, :, pl.ds(0, most)], sx)
    done(mapin.at[pl.ds(0, LEN - TOK), :], smap)
    done(stin.at[pl.ds(0, NHEAD - 1)], sstep)
    done(pkall.at[pl.ds(0, 3)], spar)
    done(xin.at[0, pl.ds(0, BATCH * EDGE), :], shx)
    done(mapin.at[pl.ds(0, EDGE), :], shm)
    done(mapc.at[0], ssib)
    done(zs1.at[pl.ds(0, BATCH * (NSEQ - 1))], sz1)
    done(zs2.at[pl.ds(0, BATCH * (NSEQ - 1))], sz2)
    done(out.at[:, :, pl.ds(0, most)], sout)
    done(out, rout)


def local(proj, maps, step, sb, dr, sg, cw, cb, mw, mb):
    hbm = pl.BlockSpec(memory_space=pltpu.HBM)
    dma = pltpu.SemaphoreType.DMA
    scratch = [
        pltpu.VMEM(step.shape, BF16),
        pltpu.VMEM((1, 8), F32),
        pltpu.VMEM((1, 8), F32),
        pltpu.VMEM((1, 8), F32),
        pltpu.VMEM(cw.shape, BF16),
        pltpu.VMEM((1, 512), F32),
        pltpu.VMEM(mw.shape, BF16),
        pltpu.VMEM((1, 4096), F32),
        pltpu.VMEM((BATCH, EDGE + LEN, CH), BF16),
        pltpu.VMEM((EDGE + LEN, CH), BF16),
        pltpu.VMEM((2, LEN, CH), BF16),
        pltpu.VMEM((SPANS, 256, SPAN), BF16),
        pltpu.VMEM((SPANS, SPAN, SPAN), F32),
        pltpu.VMEM((2, LEN, CH), BF16),
        pltpu.VMEM((2, SPANS, 256, CH), F32),
        pltpu.VMEM((2, LEN, CH), F32),
        pltpu.VMEM((BATCH, LEN, CH), BF16),
        pltpu.VMEM((2, 64 + EDGE, 128), F32),
        pltpu.VMEM((2, 256, 128), BF16),
        pltpu.VMEM((NHEAD, 16, 128), BF16),
        pltpu.VMEM((16, LEN), F32),
        pltpu.VMEM((8, 768), F32),
        pltpu.VMEM((4, 8, 768), F32),
        pltpu.VMEM((SPANS, 16, SPAN), F32),
        pltpu.VMEM((SPANS, 16, SPAN), F32),
        pltpu.VMEM((7, 16, SPAN), F32),
        pltpu.VMEM((SPANS, BATCH, 32, SPAN), F32),
        pltpu.VMEM((SPANS, BATCH, 8, SPAN), F32),
        pltpu.VMEM((BATCH * NSEQ, 48, CH), BF16),
        pltpu.VMEM((BATCH, NSEQ, 48, CH), BF16),
        pltpu.VMEM((BATCH * NSEQ, 32, CH), BF16),
        pltpu.VMEM((BATCH, 256, CH), BF16),
        pltpu.VMEM((2, SPANS, 8, CH), F32),
        pltpu.VMEM((SPANS, 8, CH), F32),
    ]
    scratch += [dma((8,))] + [dma((BATCH,))] * 4 + [dma] * 16
    pin = lambda a: pltpu.with_memory_space_constraint(a, pltpu.HBM)
    return pl.pallas_call(
        kernel,
        out_shape=jax.ShapeDtypeStruct(proj.shape, BF16),
        in_specs=[hbm] * 10,
        out_specs=pl.BlockSpec(memory_space=pl.ANY),
        scratch_shapes=scratch,
        compiler_params=pltpu.CompilerParams(
            collective_id=0, has_side_effects=True, vmem_limit_bytes=48 * 1024 * 1024
        ),
    )(
        *[pin(a) for a in (proj, maps, step, sb.reshape(1, -1), dr.reshape(1, -1), sg.reshape(1, -1),
        cw, cb.reshape(1, -1), mw, mb.reshape(1, -1))],
    )


def solution(mesh):
    return jax.shard_map(
        local,
        mesh=mesh,
        in_specs=(
            P(None, ("seq", "head"), None),
            P(None, ("seq", "head"), None),
            P(None, ("seq", "head"), None),
            P("head"),
            P("head"),
            P("head"),
            P(None, "head"),
            P("head"),
            P(),
            P(),
        ),
        out_specs=P(None, ("seq", "head"), None),
        check_vma=False,
    )
```

```python
import jax
import jax.numpy as jnp
from jax import lax
from jax.experimental import pallas as pl
from jax.experimental.pallas import tpu as pltpu
from jax.sharding import PartitionSpec as P

MESH = pl.DeviceIdType.MESH
F32 = jnp.float32
BF16 = jnp.bfloat16
SPAN = 256
TOK = 64
LEN = 2048
SPANS = LEN // SPAN
NHEAD = 32
NSEQ = 8
BATCH = 4
CH = 256
STRIDE = 5
EDGE = 16
DI = 16384
LOG2E = 1.4426950408889634
CAP = 64.0


def dot(a, b):
    return jnp.dot(a, b, preferred_element_type=F32)


def split(v):
    high = v.astype(BF16).astype(F32)
    rest = v - high
    middle = rest.astype(BF16).astype(F32)
    return high, middle, rest - middle


def silu(v):
    return v / (1.0 + jnp.exp(-v))


def kernel(
    proj, maps, step_in, sb_in, dr_in, sg_in, cw_in, cb_in, mw_in, mb_in, out,
    step, sb, dr, sg, cw, cb, mw, mb,
    xin, mapin, mapc, bt, sc, xi, hs, intra, ob, win, stt, stin, stf, pk, pkall,
    cumr, delr, work, rs, b2, zs1, zr1, zs2, hin, wrow, grow,
    small, rx, rhx, rz1, rz2, rmap, rstep, rpar, rhm, rsib, rout,
    sx, smap, sstep, spar, shx, shm, ssib, sz1, sz2, sout,
):
    h = lax.axis_index("head")
    z = lax.axis_index("seq")
    g = h // 4
    r = lax.rem(h, 4)
    c = lax.rem(h, 2)
    seq = r // 2
    hb = g * 2 + c

    def peer(i):
        return lax.rem(h + i * STRIDE, NHEAD)

    def zpeer(i):
        return lax.rem(z + i, NSEQ)

    barrier = pltpu.get_barrier_semaphore()

    def greet(i, carry):
        pl.semaphore_signal(barrier, 1, device_id=(z, peer(i)), device_id_type=MESH)
        return carry

    def greet_z(i, carry):
        pl.semaphore_signal(barrier, 1, device_id=(zpeer(i), h), device_id_type=MESH)
        return carry

    lax.fori_loop(1, NHEAD, greet, 0)
    lax.fori_loop(1, NSEQ, greet_z, 0)
    def cols(start, width=CH):
        return pl.ds(pl.multiple_of(start, 128), width)

    def rows(start, count):
        return pl.ds(pl.multiple_of(start, 16), count)

    def map_src(d):
        return maps.at[lax.rem(d // 2, 2), :, cols(lax.rem(d, 2) * 2048 + (d // 4) * 256)]

    def x_src(d, b):
        base = ((d // 4) * 2 + lax.rem(d, 2)) * 1024
        return proj.at[lax.rem(d // 2, 2), :, cols(base + b * CH)]

    def st_src(d):
        return stt.at[lax.rem(d // 2, 2), rows(((d // 4) * 2 + lax.rem(d, 2)) * 16, 16), :]

    map_dst = mapin.at[rows(EDGE + h * TOK, TOK), :]

    def send_map(i, carry):
        d = peer(i)
        pltpu.make_async_remote_copy(
            map_src(d), map_dst, smap, rmap, device_id=(z, d), device_id_type=MESH
        ).start()
        return carry

    def send_x(b):
        dst = xin.at[b, rows(EDGE + h * TOK, TOK), :]
        pltpu.make_async_copy(x_src(h, b), dst, rx.at[b]).start()

        def one(i, carry):
            d = peer(i)
            pltpu.make_async_remote_copy(
                x_src(d, b), dst, sx, rx.at[b], device_id=(z, d), device_id_type=MESH
            ).start()
            return carry

        lax.fori_loop(1, NHEAD, one, 0)

    arrivals = [
        pltpu.make_async_copy(src, dst, small.at[i])
        for i, (src, dst) in enumerate(
            [(step_in, step), (sb_in, sb), (dr_in, dr), (sg_in, sg), (cw_in, cw), (cb_in, cb),
             (mw_in, mw), (mb_in, mb)]
        )
    ]
    for arrival in arrivals:
        arrival.start()
    pl.semaphore_wait(barrier, NHEAD - 1 + NSEQ - 1)
    pltpu.make_async_copy(map_src(h), map_dst, rmap).start()
    lax.fori_loop(1, NHEAD, send_map, 0)
    for arrival in arrivals:
        arrival.wait()

    eye = lax.broadcasted_iota(jnp.int32, (8, 8), 0) == lax.broadcasted_iota(jnp.int32, (8, 8), 1)

    def column(ref):
        return jnp.sum(jnp.where(eye, jnp.broadcast_to(ref[...], (8, 8)), 0.0), axis=1, keepdims=True)

    owner = lax.broadcasted_iota(jnp.int32, (8, 512), 1) // 64 == lax.broadcasted_iota(
        jnp.int32, (8, 512), 0
    )
    pk[0:4, 0:512] = cw[...].astype(F32)
    pk[4:5, 0:512] = cb[...]
    pk[5:6, 0:512] = jnp.sum(jnp.where(owner, column(sg), 0.0), axis=0, keepdims=True)
    pk[6:8, 0:512] = jnp.zeros((2, 512), F32)
    pk[:, 512:640] = jnp.broadcast_to(column(sb), (8, 128))
    pk[:, 640:768] = jnp.broadcast_to(column(dr), (8, 128))

    half = lax.broadcasted_iota(jnp.int32, (2 * TOK, 256), 0) // TOK == c
    for s in range(2):
        v = step[s].astype(F32)
        v = jnp.where(half, jnp.concatenate([v, v], axis=0), 0.0)
        stt[s] = v.T.astype(BF16)

    def send_step(i, carry):
        d = peer(i)
        pltpu.make_async_remote_copy(
            st_src(d), stin.at[h], sstep, rstep, device_id=(z, d), device_id_type=MESH
        ).start()
        return carry

    pltpu.make_async_copy(pk, pkall.at[r], rpar).start()
    for i in range(1, 4):
        pltpu.make_async_remote_copy(
            pk, pkall.at[r], spar, rpar, device_id=(z, g * 4 + lax.rem(r + i, 4)), device_id_type=MESH
        ).start()
    pltpu.make_async_copy(st_src(h), stin.at[h], rstep).start()
    lax.fori_loop(1, NHEAD, send_step, 0)
    for b in range(BATCH):
        send_x(b)

    def done(ref, sem):
        pltpu.make_async_copy(ref, ref, sem).wait()

    def conv(src, k, weight, bias, store):
        def part(i, carry):
            start = pl.multiple_of(k * SPAN + i * 64, 16)
            for j in range(2):
                lanes = slice(j * 128, (j + 1) * 128)
                win[j] = src[pl.ds(start, 64 + EDGE), lanes].astype(F32)
                total = bias[:, lanes]
                for tap in range(4):
                    total = total + weight[tap : tap + 1, lanes] * win[j, 13 + tap : 77 + tap, :]
                store(start, lanes, silu(total).astype(BF16))
            return carry

        lax.fori_loop(0, SPAN // 64, part, 0)

    def edge(buffer, send_sem, recv_sem):
        return pltpu.make_async_remote_copy(
            buffer.at[pl.ds(LEN, EDGE), :], buffer.at[pl.ds(0, EDGE), :],
            send_sem, recv_sem, device_id=(zpeer(1), h), device_id_type=MESH,
        )

    def first_block(buffer):
        @pl.when(z == 0)
        def _():
            buffer[0:EDGE, :] = jnp.zeros((EDGE, CH), BF16)

    done(pkall, rpar)
    done(stin, rstep)
    for i in range(16):
        stf[:, i * 128 : (i + 1) * 128] = stin[2 * i].astype(F32) + stin[2 * i + 1].astype(F32)
    bias_col = jnp.concatenate([pkall[2 * c, :, 512:513], pkall[2 * c + 1, :, 512:513]], axis=0)
    rate_col = jnp.concatenate([pkall[2 * c, :, 640:641], pkall[2 * c + 1, :, 640:641]], axis=0)
    upper = (
        lax.broadcasted_iota(jnp.int32, (SPAN, SPAN), 0)
        <= lax.broadcasted_iota(jnp.int32, (SPAN, SPAN), 1)
    ).astype(BF16)
    for k in range(SPANS):
        v = stf[:, k * SPAN : (k + 1) * SPAN] + bias_col
        delta = jnp.maximum(v, 0.0) + jnp.log1p(jnp.exp(-jnp.abs(v)))
        delr[k] = delta
        first, second, third = split(-delta * rate_col * LOG2E)
        cumr[k] = (
            dot(first.astype(BF16), upper) + dot(second.astype(BF16), upper)
        ) + dot(third.astype(BF16), upper)

    def rows_of(k, carry):
        cum = cumr[k]
        delta = delr[k]
        scale = jnp.exp2(cum[:, SPAN - 1 :] - cum) * delta
        s_high, s_low, _ = split(scale)
        e_high, e_mid, e_low = split(jnp.exp2(cum))
        work[0] = cum
        work[1] = s_high
        work[2] = s_low
        work[3] = e_high
        work[4] = e_mid
        work[5] = e_low
        work[6] = jnp.log(delta) * LOG2E - cum
        blank = jnp.zeros((4, SPAN), F32)
        for b in range(BATCH):
            at = slice(4 * b, 4 * b + 4)
            rs[k, b, 0:4] = work[0, at]
            rs[k, b, 4:8] = blank
            rs[k, b, 8:12] = work[1, at]
            rs[k, b, 12:16] = work[2, at]
            rs[k, b, 16:20] = work[3, at]
            rs[k, b, 20:24] = work[4, at]
            rs[k, b, 24:28] = work[5, at]
            rs[k, b, 28:32] = blank
            b2[k, b, 0:4] = work[6, at]
            b2[k, b, 4:8] = blank
        return carry

    lax.fori_loop(0, SPANS, rows_of, 0)

    done(mapin.at[pl.ds(EDGE, LEN), :], rmap)
    edge(mapin, shm, rhm).start()
    done(mapin.at[pl.ds(0, EDGE), :], rhm)
    first_block(mapin)
    which = cols(c * 2048 + g * 256)
    map_weight = mw[:, which].astype(F32)
    map_bias = mb[:, which]

    def map_span(k, carry):
        def store(start, lanes, value):
            mapc[c, pl.ds(start, 64), lanes] = value

        conv(mapin, k, map_weight, map_bias, store)
        return carry

    lax.fori_loop(0, SPANS, map_span, 0)
    sibling = pltpu.make_async_remote_copy(
        mapc.at[c], mapc.at[c], ssib, rsib, device_id=(z, g * 4 + seq * 2 + 1 - c), device_id_type=MESH
    )
    sibling.start()

    causal = lax.broadcasted_iota(jnp.int32, (SPAN, SPAN), 0) >= lax.broadcasted_iota(
        jnp.int32, (SPAN, SPAN), 1
    )

    def scores(k, carry):
        at = pl.ds(pl.multiple_of(k * SPAN, SPAN), SPAN)
        bt[k] = mapc[0, at, :].astype(F32).T.astype(BF16)
        sc[k] = jnp.where(causal, dot(mapc[1, at, :], bt[k]), 0.0)
        return carry


    row_id = lax.broadcasted_iota(jnp.int32, (32, CH), 0)
    same = lax.rem(row_id, 4) == lax.broadcasted_iota(jnp.int32, (32, CH), 1) // 64
    pick_scale = (same & (row_id >= 8) & (row_id < 16)).astype(BF16)
    pick_decay = (same & (row_id >= 16) & (row_id < 28)).astype(BF16)
    low_lanes = lax.broadcasted_iota(jnp.int32, (SPAN // 2, 128), 1) < 64

    def params_of(b):
        return pkall.at[2 * c + b // 2, :, cols(lax.rem(b, 2) * CH)]

    def convolve(b):
        two = lax.rem(b, 2)
        par = params_of(b)
        weight = par[0:4, :]
        bias = par[4:5, :]
        done(xin.at[b, pl.ds(EDGE, LEN), :], rx.at[b])
        edge(xin.at[b], shx, rhx.at[b]).start()

        def store(start, lanes, value):
            xi[two, pl.ds(start, 64), lanes] = value

        def span(k, carry):
            conv(xin.at[b], k, weight, bias, store)
            return carry

        lax.fori_loop(1, SPANS, span, 0)
        done(xin.at[b, pl.ds(0, EDGE), :], rhx.at[b])
        first_block(xin.at[b])
        span(0, 0)

    def states(b):
        two = lax.rem(b, 2)

        def produce(k):
            at = pl.ds(pl.multiple_of(k * SPAN, SPAN), SPAN)
            stack = rs[k, b].T.astype(BF16)
            scale = dot(stack, pick_scale)
            growth = dot(stack[SPAN - 16 :], pick_decay)[15:16]
            carried = (xi[two, at, :].astype(F32) * scale).astype(BF16)
            hs[two, k] = dot(bt[k], carried)
            grow[k] = jnp.broadcast_to(growth, (8, CH))

        def spans(i, carry):
            produce(2 * i)
            produce(2 * i + 1)
            return carry

        lax.fori_loop(0, SPANS // 2, spans, 0)
        total = jnp.ones((8, CH), F32)
        for k in range(SPANS):
            wrow[two, k] = total
            total = total * grow[k]
        first, second, third = split(total[0:1])
        line = lax.broadcasted_iota(jnp.int32, (16, CH), 0)
        growth_rows = jnp.where(
            line == 0, first, jnp.where(line == 1, second, jnp.where(line == 2, third, 0.0))
        ).astype(BF16)

        def scan(j, carry):
            part = pl.ds(pl.multiple_of(j * 32, 32), 32)
            state = jnp.zeros((32, CH), F32)
            for k in range(SPANS):
                made = hs[two, k, part, :]
                hs[two, k, part, :] = state
                state = grow[k, 0:1] * state + made
            zs1[b * NSEQ + j, 0:32, :] = state.astype(BF16)
            zs1[b * NSEQ + j, 32:48, :] = growth_rows
            return carry

        lax.fori_loop(0, NSEQ, scan, 0)
        def send(i, carry):
            d = zpeer(i)
            pltpu.make_async_remote_copy(
                zs1.at[b * NSEQ + d], zr1.at[b, z], sz1, rz1.at[b], device_id=(d, h), device_id_type=MESH
            ).start()
            return carry

        @pl.when(z < NSEQ - 1)
        def _():
            pltpu.make_async_copy(zs1.at[b * NSEQ + z], zr1.at[b, z], rz1.at[b]).start()
            lax.fori_loop(1, NSEQ, send, 0)

    def relay(b):
        done(zr1.at[b, pl.ds(0, NSEQ - 1)], rz1.at[b])
        state = jnp.zeros((32, CH), F32)
        for j in range(NSEQ):
            zs2[b * NSEQ + j] = state.astype(BF16)
            if j == NSEQ - 1:
                break
            growth = zr1[b, j, 32:48, :].astype(F32)
            growth = growth[0:1] + growth[1:2] + growth[2:3]
            state = growth * state + zr1[b, j, 0:32, :].astype(F32)
        here = hin.at[b, pl.ds(pl.multiple_of(z * 32, 32), 32), :]
        pltpu.make_async_copy(zs2.at[b * NSEQ + z], here, rz2.at[b]).start()

        def send(i, carry):
            d = zpeer(i)
            pltpu.make_async_remote_copy(
                zs2.at[b * NSEQ + d], here, sz2, rz2.at[b], device_id=(d, h), device_id_type=MESH
            ).start()
            return carry

        lax.fori_loop(1, NSEQ, send, 0)

    HALF = SPAN // 2

    def within(b):
        two = lax.rem(b, 2)
        skip = params_of(b)[5:6, :]

        def one_span(k):
            columns = rs[k, b, 0:8].T
            for pair in range(2):
                lanes = slice(pair * 128, (pair + 1) * 128)
                at = pl.ds(pl.multiple_of(k * SPAN, SPAN), SPAN)
                x_pair = xi[two, at, lanes]
                early = []
                late = []
                for one in range(2):
                    i = pair * 2 + one
                    row = b2[k, b, i : i + 1]
                    a_early = columns[:HALF, i : i + 1]
                    a_late = columns[HALF:, i : i + 1]
                    w = jnp.exp2(jnp.minimum(a_early + row[:, :HALF], CAP)) * sc[k, :HALF, :HALF]
                    early.append(dot(w.astype(BF16), x_pair[:HALF]))
                    w_old = jnp.exp2(a_late + row[:, :HALF]) * sc[k, HALF:, :HALF]
                    w_own = jnp.exp2(jnp.minimum(a_late + row[:, HALF:], CAP)) * sc[k, HALF:, HALF:]
                    w = jnp.concatenate([w_old.astype(BF16), w_own.astype(BF16)], axis=1)
                    late.append(dot(w, x_pair))
                direct = skip[:, lanes] * x_pair.astype(F32)
                start = pl.multiple_of(k * SPAN, SPAN)
                intra[two, pl.ds(start, HALF), lanes] = (
                    jnp.where(low_lanes, early[0], early[1]) + direct[:HALF]
                )
                intra[two, pl.ds(start + HALF, HALF), lanes] = (
                    jnp.where(low_lanes, late[0], late[1]) + direct[HALF:]
                )

        def spans(i, carry):
            one_span(2 * i)
            one_span(2 * i + 1)
            return carry

        lax.fori_loop(0, SPANS // 2, spans, 0)

    def finish(b):
        two = lax.rem(b, 2)
        done(hin.at[b], rz2.at[b])

        def span(k):
            at = pl.ds(pl.multiple_of(k * SPAN, SPAN), SPAN)
            entering = (hs[two, k] + wrow[two, k, 0:1] * hin[b].astype(F32)).astype(BF16)
            inter = dot(mapc[1, at, :], entering)
            decay = dot(rs[k, b].T.astype(BF16), pick_decay)
            ob[b, at, :] = (intra[two, at, :] + decay * inter).astype(BF16)

        def spans(i, carry):
            span(2 * i)
            span(2 * i + 1)
            return carry

        lax.fori_loop(0, SPANS // 2, spans, 0)
        dst = out.at[seq, :, cols(hb * 1024 + b * CH)]

        def leave(i, carry):
            d = peer(i)
            pltpu.make_async_remote_copy(
                ob.at[b, rows(d * TOK, TOK), :], dst, sout, rout, device_id=(z, d), device_id_type=MESH
            ).start()
            return carry

        pltpu.make_async_copy(ob.at[b, rows(h * TOK, TOK), :], dst, rout).start()
        lax.fori_loop(1, NHEAD, leave, 0)

    def turn(i, carry):
        @pl.when(i > 0)
        def _():
            relay(i - 1)

        @pl.when(i < BATCH)
        def _():
            convolve(i)

        @pl.when(i == 0)
        def _():
            done(mapc.at[1 - c], rsib)
            lax.fori_loop(0, SPANS, scores, 0)

        @pl.when(i < BATCH)
        def _():
            states(i)

        @pl.when(i > 0)
        def _():
            finish(i - 1)

        @pl.when(i < BATCH)
        def _():
            within(i)

        return carry

    lax.fori_loop(0, BATCH + 1, turn, 0)

    most = DI - DI // NHEAD
    done(proj.at[:, :, pl.ds(0, most)], sx)
    done(mapin.at[pl.ds(0, LEN - TOK), :], smap)
    done(stin.at[pl.ds(0, NHEAD - 1)], sstep)
    done(pkall.at[pl.ds(0, 3)], spar)
    done(xin.at[0, pl.ds(0, BATCH * EDGE), :], shx)
    done(mapin.at[pl.ds(0, EDGE), :], shm)
    done(mapc.at[0], ssib)

    @pl.when(z < NSEQ - 1)
    def _():
        done(zs1.at[pl.ds(0, BATCH * (NSEQ - 1))], sz1)

    done(zs2.at[pl.ds(0, BATCH * (NSEQ - 1))], sz2)
    done(out.at[:, :, pl.ds(0, most)], sout)
    done(out, rout)


def local(proj, maps, step, sb, dr, sg, cw, cb, mw, mb):
    hbm = pl.BlockSpec(memory_space=pltpu.HBM)
    dma = pltpu.SemaphoreType.DMA
    scratch = [
        pltpu.VMEM(step.shape, BF16),
        pltpu.VMEM((1, 8), F32),
        pltpu.VMEM((1, 8), F32),
        pltpu.VMEM((1, 8), F32),
        pltpu.VMEM(cw.shape, BF16),
        pltpu.VMEM((1, 512), F32),
        pltpu.VMEM(mw.shape, BF16),
        pltpu.VMEM((1, 4096), F32),
        pltpu.VMEM((BATCH, EDGE + LEN, CH), BF16),
        pltpu.VMEM((EDGE + LEN, CH), BF16),
        pltpu.VMEM((2, LEN, CH), BF16),
        pltpu.VMEM((SPANS, 256, SPAN), BF16),
        pltpu.VMEM((SPANS, SPAN, SPAN), F32),
        pltpu.VMEM((2, LEN, CH), BF16),
        pltpu.VMEM((2, SPANS, 256, CH), F32),
        pltpu.VMEM((2, LEN, CH), F32),
        pltpu.VMEM((BATCH, LEN, CH), BF16),
        pltpu.VMEM((2, 64 + EDGE, 128), F32),
        pltpu.VMEM((2, 256, 128), BF16),
        pltpu.VMEM((NHEAD, 16, 128), BF16),
        pltpu.VMEM((16, LEN), F32),
        pltpu.VMEM((8, 768), F32),
        pltpu.VMEM((4, 8, 768), F32),
        pltpu.VMEM((SPANS, 16, SPAN), F32),
        pltpu.VMEM((SPANS, 16, SPAN), F32),
        pltpu.VMEM((7, 16, SPAN), F32),
        pltpu.VMEM((SPANS, BATCH, 32, SPAN), F32),
        pltpu.VMEM((SPANS, BATCH, 8, SPAN), F32),
        pltpu.VMEM((BATCH * NSEQ, 48, CH), BF16),
        pltpu.VMEM((BATCH, NSEQ, 48, CH), BF16),
        pltpu.VMEM((BATCH * NSEQ, 32, CH), BF16),
        pltpu.VMEM((BATCH, 256, CH), BF16),
        pltpu.VMEM((2, SPANS, 8, CH), F32),
        pltpu.VMEM((SPANS, 8, CH), F32),
    ]
    scratch += [dma((8,))] + [dma((BATCH,))] * 4 + [dma] * 16
    pin = lambda a: pltpu.with_memory_space_constraint(a, pltpu.HBM)
    return pl.pallas_call(
        kernel,
        out_shape=jax.ShapeDtypeStruct(proj.shape, BF16),
        in_specs=[hbm] * 10,
        out_specs=pl.BlockSpec(memory_space=pl.ANY),
        scratch_shapes=scratch,
        compiler_params=pltpu.CompilerParams(
            collective_id=0, has_side_effects=True, vmem_limit_bytes=48 * 1024 * 1024
        ),
    )(
        *[pin(a) for a in (proj, maps, step, sb.reshape(1, -1), dr.reshape(1, -1), sg.reshape(1, -1),
        cw, cb.reshape(1, -1), mw, mb.reshape(1, -1))],
    )


def solution(mesh):
    return jax.shard_map(
        local,
        mesh=mesh,
        in_specs=(
            P(None, ("seq", "head"), None),
            P(None, ("seq", "head"), None),
            P(None, ("seq", "head"), None),
            P("head"),
            P("head"),
            P("head"),
            P(None, "head"),
            P("head"),
            P(),
            P(),
        ),
        out_specs=P(None, ("seq", "head"), None),
        check_vma=False,
    )
```
